32 devices in a mesh: groups: 2 (over y), seq: 4 (over z), head: 4 (over x, core).
Axes of the slice: x: 2, y: 2, z: 4, core: 2. Of those that a mesh axis runs over, the one named last changes fastest.
Arguments:
- layer_queries: bfloat16 [4096, 4096], P(('groups', 'seq'), 'head'), parts along dimension 0, may hold values from -1.75 to 1.75
- layer_keys: bfloat16 [4096, 4096], P(('groups', 'seq'), 'head'), parts along dimension 0, may hold values from -1.75 to 1.75
- layer_values: bfloat16 [4096, 4096], P(('groups', 'seq'), 'head'), parts along dimension 0, may hold values from -6 to 6
- gate_logits: bfloat16 [4096, 4096], P(('groups', 'seq'), 'head'), parts along dimension 0, may hold values from -6 to 6
- norm_gain: bfloat16 [4096], P('head'), may hold values from 0.099609375 to 1.8984375
- decay_exponents: int32 [32], P('head'), may hold values from 0 to 9
- doc_lengths: int32 [8], P('groups'), parts along dimension 0, may hold values from 1 to 1024, 2048 in all
- out_weight: bfloat16 [6144, 4096], P('seq', 'head'), may hold values from -0.125 to 0.125
Outputs:
- layer_output: bfloat16 [4096, 6144], P(('groups', 'seq'), 'head'), parts along dimension 0
The draws below stay inside these ranges and needn't reach their ends.
There are 2 independent parts, one for each index of `groups`. The reference program is written for one: setup_inputs(seed, part) draws one part's arguments, and reference() takes and returns one part's arrays. A program takes and returns all parts, laid end to end along the dimension named above; an argument that names none is the same for every part. Nothing has to cross between parts.
Inputs may be any that keep to these rules, and one draw needn't show every extreme that they name: `doc_lengths`: the lengths sum to 2048.
All inputs are finite; a program needn't handle non-finite values.
Results may differ from the reference program's by a relative error of at most 0.0063.
Values may be sent and summed in bfloat16 or wider, within the bound.
A program may use at most 128 MiB of HBM per device.

```python
import math
import jax
import jax.numpy as jnp
import numpy as np
from jax import lax

D = 6144
HEAD_DIM = 128
HEADS = 32
TOK_DEV = 512
DOCS = 4
TOKENS = 2048
N_SEQ = 4


def draw_decay_exponents(key, part):
    first_key, second_key, third_key, fourth_key = jax.random.split(key, 4)
    picker = jax.random.randint(first_key, (HEADS,), 0, 2)
    slower = jax.random.randint(second_key, (HEADS,), 0, 2)
    faster = jax.random.randint(third_key, (HEADS,), 6, 10)
    chosen = picker * slower + (1 - picker) * faster
    shuffled = jax.random.permutation(fourth_key, HEADS)
    chosen = chosen.at[shuffled[0]].set(0).at[shuffled[1]].set(9)
    return chosen.astype(jnp.int32)


def spiked(values, stream_key, source, target, parts, factor):
    def block_of(dim):
        return (jnp.arange(values.shape[dim]) // (values.shape[dim] // parts)).reshape((-1,) + (1,) * (values.ndim - 1 - dim))

    first = jax.random.permutation(stream_key, parts)[block_of(target)]
    second = (block_of(target) + parts // 2) % parts
    return jnp.where((block_of(source) == first) | (block_of(source) == second), factor * values, values)


def levels(own_key, dims, pieces, smallest, top_value):
    level, own = 1.0, jax.random.fold_in(own_key, 6)
    for dim, blocks in pieces:
        draws = jnp.exp(jax.random.uniform(jax.random.fold_in(own, dim), (blocks,), jnp.float32, smallest / len(pieces), top_value / len(pieces)))
        level = level * jnp.repeat(draws, dims[dim] // blocks).reshape([-1 if axis == dim else 1 for axis in range(len(dims))])
    return level


def split_up(amount, total, most, slope):
    loads = [(1 << 20) // math.isqrt(rank ** slope) + 1 for rank in range(2, amount + 1)]
    rest, counts = total - most - (amount - 1), [1] * (amount - 1)
    while rest > 0:
        free = [i for i in range(amount - 1) if counts[i] < most]
        whole, left = sum([loads[i] for i in free]), rest
        for i in free:
            addition = min(most - counts[i], max(1, left * loads[i] // whole), rest)
            counts[i] = counts[i] + addition
            rest = rest - addition
    return np.array([most] + counts)


def uneven(own_key, count, total, limit, skew):
    if count == 2:
        one = jax.random.randint(own_key, (), max(1, total - limit), min(limit, total - 1) + 1)
        return jnp.stack([one, total - one])
    tallies = jnp.asarray(split_up(count, total, limit, skew), jnp.int32)
    couples = (count - 1) // 2
    giver, receiver = tallies[1:1 + 2 * couples:2], tallies[2:2 + 2 * couples:2]
    slack = jnp.minimum(giver - 1, limit - receiver)
    moved = jax.random.randint(jax.random.fold_in(own_key, 1), (couples,), 0, 1 << 20) % (slack + 1)
    tallies = tallies.at[1:1 + 2 * couples:2].set(giver - moved).at[2:2 + 2 * couples:2].set(receiver + moved)
    return tallies[jax.random.permutation(jax.random.fold_in(own_key, 2), count)]


def gaussian(own_key, extent, scale, bound, cuts=(), kind=jnp.bfloat16):
    drawn = jax.random.normal(own_key, extent, jnp.float32) * scale
    if len(cuts) > 0:
        drawn = levels(own_key, extent, cuts, -0.22, 0.18) * drawn
    return jnp.clip(drawn, min=-bound, max=bound).astype(kind)


def bell_draw_with(key, dims, width, limit, pieces, heavy, kind=jnp.bfloat16):
    array = width * jax.random.normal(key, dims, jnp.float32)
    if pieces:
        array = array * levels(key, dims, pieces, -0.22, 0.18)
    return jnp.clip(spiked(array, jax.random.fold_in(key, 3), *heavy), -limit, limit).astype(kind)


def setup_inputs(seed: int = 0, part: int = 0) -> dict:
    keys = jax.random.split(jax.random.key(seed), 9)
    own_keys = jax.random.split(jax.random.fold_in(keys[8], part), 9)
    layer_queries = gaussian(own_keys[0], (TOKENS, HEADS * HEAD_DIM), 0.3, 1.75, ((0, 4), (1, 4)))
    layer_keys = gaussian(own_keys[1], (TOKENS, HEADS * HEAD_DIM), 0.3, 1.75, ((0, 4), (1, 4)))
    layer_values = gaussian(own_keys[2], (TOKENS, HEADS * HEAD_DIM), 1.0, 6.0, ((0, 4), (1, 4)))
    gate_logits = gaussian(own_keys[3], (TOKENS, HEADS * HEAD_DIM), 1.0, 6.0, ((0, 4), (1, 4)))
    norm_gain = jnp.clip(1.0 + 0.18 * jax.random.normal(keys[4], (HEADS * HEAD_DIM,), jnp.float32), 0.099609375, 1.8984375).astype(jnp.bfloat16)
    decay_exponents = draw_decay_exponents(jax.random.fold_in(keys[8], 71), part)
    doc_lengths = uneven(own_keys[6], DOCS, TOKENS, TOKENS // 2, 0).astype(jnp.int32)
    out_weight = bell_draw_with(keys[7], (D, HEADS * HEAD_DIM), (HEADS * HEAD_DIM) ** -0.5, 0.125, ((0, 4), (1, 4)), (1, 0, 4, 2.0))
    return {"layer_queries": layer_queries, "layer_keys": layer_keys, "layer_values": layer_values, "gate_logits": gate_logits, "norm_gain": norm_gain, "decay_exponents": decay_exponents, "doc_lengths": doc_lengths, "out_weight": out_weight}


def doc_positions(doc_lengths, first_row, count):
    position = first_row + jnp.arange(count, dtype=jnp.int32)
    starts = (jnp.cumsum(doc_lengths) - doc_lengths).astype(jnp.int32)
    doc_begin = lax.optimization_barrier(jnp.max(jnp.where(starts[None, :] <= position[:, None], starts[None, :], 0), axis=1))
    return (position - doc_begin).astype(jnp.int32)

def reference(layer_queries, layer_keys, layer_values, gate_logits, norm_gain, decay_exponents, doc_lengths, out_weight):
    decay_rate = jnp.minimum(jnp.exp2(decay_exponents.astype(jnp.float32)) / TOKENS, 1.0 / 32.0)
    within = doc_positions(doc_lengths, 0, TOKENS).reshape(N_SEQ, TOK_DEV)
    query_blocks = layer_queries.reshape(N_SEQ, TOK_DEV, HEADS, HEAD_DIM)
    key_blocks = layer_keys.reshape(N_SEQ, TOK_DEV, HEADS, HEAD_DIM)
    value_blocks = layer_values.reshape(N_SEQ, TOK_DEV, HEADS, HEAD_DIM)
    gate_blocks = gate_logits.reshape(N_SEQ, TOK_DEV, HEADS * HEAD_DIM)
    local_pos = jnp.arange(TOK_DEV, dtype=jnp.int32)
    lag_grid = local_pos[:, None] - local_pos[None, :]

    def block_step(kv_state, block_data):
        query_block, key_block, value_block, gate_block, within_block = block_data
        valid_mask = (lag_grid >= 0) & (lag_grid <= within_block[:, None])
        decay_grid = jnp.where(valid_mask[None], jnp.exp(-decay_rate[:, None, None] * lag_grid[None].astype(jnp.float32)), 0.0)
        scores = jnp.einsum('thd,shd->hts', query_block.astype(jnp.float32), key_block.astype(jnp.float32))
        weights = (scores * decay_grid).astype(jnp.bfloat16)
        intra_attn = jnp.einsum('hts,shd->thd', weights.astype(jnp.float32), value_block.astype(jnp.float32))
        query_weight = jnp.where((within_block >= local_pos + 1)[:, None], jnp.exp(-decay_rate[None, :] * local_pos[:, None].astype(jnp.float32)), 0.0)
        state_rounded = kv_state.astype(jnp.bfloat16)
        cross_attn = jnp.einsum('thd,hde->the', query_block.astype(jnp.float32), state_rounded.astype(jnp.float32)) * query_weight[:, :, None]
        attention = (intra_attn + cross_attn).reshape(TOK_DEV, HEADS * HEAD_DIM)
        last_within = within_block[TOK_DEV - 1]
        carry_on = jnp.where(last_within >= TOK_DEV, jnp.exp(-decay_rate * TOK_DEV), 0.0)
        key_weight = jnp.where((local_pos >= TOK_DEV - 1 - last_within)[:, None], jnp.exp(-decay_rate[None, :] * (TOK_DEV - local_pos)[:, None].astype(jnp.float32)), 0.0)
        scaled = (key_block.astype(jnp.float32) * key_weight[:, :, None]).astype(jnp.bfloat16)
        block_state = jnp.einsum('thd,the->hde', scaled.astype(jnp.float32), value_block.astype(jnp.float32))
        new_state = carry_on[:, None, None] * kv_state + block_state
        mean_sq = lax.optimization_barrier(jnp.mean(attention * attention, axis=1))
        gated_out = (attention * lax.rsqrt(mean_sq + 1e-06)[:, None] * norm_gain.astype(jnp.float32) * jax.nn.sigmoid(gate_block.astype(jnp.float32))).astype(jnp.bfloat16)
        projected = lax.dot_general(gated_out, out_weight, (((1,), (1,)), ((), ())), preferred_element_type=jnp.float32)
        return (new_state, projected.astype(jnp.bfloat16))
    init_state = jnp.zeros((HEADS, HEAD_DIM, HEAD_DIM), jnp.float32)
    final_state, block_outs = lax.scan(block_step, init_state, (query_blocks, key_blocks, value_blocks, gate_blocks, within))
    return block_outs.reshape(TOKENS, D)
```

```python
import jax
import jax.numpy as jnp
from jax import lax
from jax.sharding import PartitionSpec as P

HEAD_DIM = 128


def prefix(value, axis, join, neutral):
    count, mine = (lax.axis_size(axis), lax.axis_index(axis))
    pieces = jax.tree.map(lambda part: lax.all_gather(part, axis), value)
    running = jax.tree.map(
        lambda part, zero: jnp.full_like(part, 0) + jnp.asarray(zero, part.dtype), value, neutral
    )

    def turn(position, running):
        longer = join(running, jax.tree.map(lambda part: part[position], pieces))
        return jax.tree.map(lambda new, old: jnp.where(position < mine, new, old), longer, running)

    return lax.fori_loop(0, count - 1, turn, running)


def doc_positions(doc_lengths, first_row, count):
    position = first_row + jnp.arange(count, dtype=jnp.int32)
    order = jnp.arange(doc_lengths.shape[0], dtype=jnp.int32)
    starts = jnp.sum(jnp.where(order[None, :] < order[:, None], doc_lengths[None, :], 0), axis=1)
    doc_begin = jnp.max(jnp.where(starts[None, :] <= position[:, None], starts[None, :], 0), axis=1)
    return position - doc_begin


def combine(earlier, latter):
    return (earlier[0] * latter[0], latter[0][:, None, None] * earlier[1] + latter[1])


def shards(
    layer_queries,
    layer_keys,
    layer_values,
    gate_logits,
    norm_gain,
    decay_exponents,
    doc_lengths,
    out_weight,
):
    tok_rows = layer_queries.shape[0]
    heads_here = decay_exponents.shape[0]
    token_span = tok_rows * lax.axis_size("seq")
    first_row = lax.axis_index("seq") * tok_rows
    decay_rate = jnp.minimum(jnp.exp2(decay_exponents.astype(jnp.float32)) / token_span, 1.0 / 32.0)
    within = doc_positions(doc_lengths, first_row, tok_rows)
    local_pos = jnp.arange(tok_rows, dtype=jnp.int32)
    query_heads = layer_queries.reshape(tok_rows, heads_here, HEAD_DIM)
    key_heads = layer_keys.reshape(tok_rows, heads_here, HEAD_DIM)
    value_heads = layer_values.reshape(tok_rows, heads_here, HEAD_DIM)
    last_within = within[tok_rows - 1]
    carry_on = jnp.where(last_within >= tok_rows, jnp.exp(-decay_rate * tok_rows), 0.0)
    key_weight = jnp.where(
        (local_pos >= tok_rows - 1 - last_within)[:, None],
        jnp.exp(-decay_rate[None, :] * (tok_rows - local_pos)[:, None].astype(jnp.float32)),
        0.0,
    )
    scaled = (key_heads.astype(jnp.float32) * key_weight[:, :, None]).astype(jnp.bfloat16)
    block_state = jnp.einsum(
        "thd,the->hde", scaled, value_heads, preferred_element_type=jnp.float32
    )
    identity = (jnp.ones_like(carry_on), jnp.zeros_like(block_state))
    incoming_decay, incoming = prefix((carry_on, block_state), "seq", combine, identity)
    lag_grid = local_pos[:, None] - local_pos[None, :]
    valid_mask = (lag_grid >= 0) & (lag_grid <= within[:, None])
    decay_grid = jnp.where(
        valid_mask[None],
        jnp.exp(-decay_rate[:, None, None] * lag_grid[None].astype(jnp.float32)),
        0.0,
    )
    scores = jnp.einsum("thd,shd->hts", query_heads, key_heads, preferred_element_type=jnp.float32)
    weights = (scores * decay_grid).astype(jnp.bfloat16)
    intra_attn = jnp.einsum(
        "hts,shd->thd", weights, value_heads, preferred_element_type=jnp.float32
    )
    incoming_rounded = incoming.astype(jnp.bfloat16)
    query_weight = jnp.where(
        (within >= local_pos + 1)[:, None],
        jnp.exp(-decay_rate[None, :] * local_pos[:, None].astype(jnp.float32)),
        0.0,
    )
    cross_attn = (
        jnp.einsum(
            "thd,hde->the", query_heads, incoming_rounded, preferred_element_type=jnp.float32
        )
        * query_weight[:, :, None]
    )
    attention = (intra_attn + cross_attn).reshape(tok_rows, heads_here * HEAD_DIM)
    squares = lax.psum(jnp.sum(attention * attention, axis=1), "head")
    width_all = heads_here * HEAD_DIM * lax.axis_size("head")
    inv_scale = lax.rsqrt(squares / width_all + 1e-06)
    gated_out = (
        attention
        * inv_scale[:, None]
        * norm_gain.astype(jnp.float32)
        * jax.nn.sigmoid(gate_logits.astype(jnp.float32))
    ).astype(jnp.bfloat16)
    partials = lax.dot_general(
        gated_out,
        lax.all_gather(out_weight, "seq", axis=0, tiled=True),
        (((1,), (1,)), ((), ())),
        preferred_element_type=jnp.float32,
    )
    return lax.psum_scatter(partials, "head", scatter_dimension=1, tiled=True).astype(jnp.bfloat16)


def solution(mesh):
    in_specs = (
        P(("groups", "seq"), "head"),
        P(("groups", "seq"), "head"),
        P(("groups", "seq"), "head"),
        P(("groups", "seq"), "head"),
        P("head"),
        P("head"),
        P("groups"),
        P("seq", "head"),
    )
    out_specs = P(("groups", "seq"), "head")
    return jax.shard_map(shards, mesh=mesh, in_specs=in_specs, out_specs=out_specs, check_vma=False)
```

```python
import jax
import jax.numpy as jnp
from jax import lax
from jax.sharding import PartitionSpec as P

HEAD_DIM = 128
CHUNKS = 2


def doc_positions(doc_lengths, position):
    order = jnp.arange(doc_lengths.shape[0], dtype=jnp.int32)
    starts = jnp.sum(jnp.where(order[None, :] < order[:, None], doc_lengths[None, :], 0), axis=1)
    doc_begin = jnp.max(jnp.where(starts[None, :] <= position[:, None], starts[None, :], 0), axis=1)
    return position - doc_begin


def shards(
    layer_queries,
    layer_keys,
    layer_values,
    gate_logits,
    norm_gain,
    decay_exponents,
    doc_lengths,
    out_weight,
):
    f32 = jnp.float32
    tok_rows = layer_queries.shape[0]
    heads_here = decay_exponents.shape[0]
    seq_count, head_count = lax.axis_size("seq"), lax.axis_size("head")
    mine = lax.axis_index("seq")
    token_span = tok_rows * seq_count
    decay_rate = jnp.minimum(jnp.exp2(decay_exponents.astype(f32)) / token_span, 1.0 / 32.0)
    local_pos = jnp.arange(tok_rows, dtype=jnp.int32)
    within = doc_positions(doc_lengths, mine * tok_rows + local_pos)
    last_within = within[tok_rows - 1]
    query_heads = layer_queries.reshape(tok_rows, heads_here, HEAD_DIM)
    key_heads = layer_keys.reshape(tok_rows, heads_here, HEAD_DIM)
    value_heads = layer_values.reshape(tok_rows, heads_here, HEAD_DIM)

    key_weight = jnp.where(
        (local_pos >= tok_rows - 1 - last_within)[:, None],
        jnp.exp(-decay_rate[None, :] * (tok_rows - local_pos)[:, None].astype(f32)),
        0.0,
    )
    scaled = (key_heads.astype(f32) * key_weight[:, :, None]).astype(jnp.bfloat16)
    block_state = jnp.einsum("thd,the->hde", scaled, value_heads, preferred_element_type=f32)
    states = lax.all_gather(block_state.astype(jnp.bfloat16), "seq")

    blocks = jnp.arange(seq_count, dtype=jnp.int32)
    ends = doc_positions(doc_lengths, blocks * tok_rows + tok_rows - 1)
    carry = jnp.where(
        (ends >= tok_rows)[:, None], jnp.exp(-decay_rate * tok_rows)[None, :], 0.0
    )
    between = (blocks[None, :] > blocks[:, None]) & (blocks[None, :] < mine)
    reach = jnp.prod(jnp.where(between[:, :, None], carry[None], 1.0), axis=1)
    reach = jnp.where((blocks < mine)[:, None], reach, 0.0)

    lag_grid = local_pos[:, None] - local_pos[None, :]
    valid_mask = (lag_grid >= 0) & (lag_grid <= within[:, None])
    decay_grid = jnp.where(
        valid_mask[None], jnp.exp(-decay_rate[:, None, None] * lag_grid[None].astype(f32)), 0.0
    )
    scores = jnp.einsum("thd,shd->hts", query_heads, key_heads, preferred_element_type=f32)
    weights = (scores * decay_grid).astype(jnp.bfloat16)
    intra_attn = jnp.einsum("hts,shd->thd", weights, value_heads, preferred_element_type=f32)
    incoming = jnp.sum(reach[:, :, None, None] * states.astype(f32), axis=0)
    query_weight = jnp.where(
        (within >= local_pos + 1)[:, None],
        jnp.exp(-decay_rate[None, :] * local_pos[:, None].astype(f32)),
        0.0,
    )
    cross_attn = (
        jnp.einsum(
            "thd,hde->the",
            query_heads,
            incoming.astype(jnp.bfloat16),
            preferred_element_type=f32,
        )
        * query_weight[:, :, None]
    )
    attention = (intra_attn + cross_attn).reshape(tok_rows, heads_here * HEAD_DIM)
    squares = lax.psum(jnp.sum(attention * attention, axis=1), "head")
    inv_scale = lax.rsqrt(squares / (heads_here * HEAD_DIM * head_count) + 1e-06)
    gated = attention * norm_gain.astype(f32) * jax.nn.sigmoid(gate_logits.astype(f32))
    contract = (((1,), (1,)), ((), ()))

    if seq_count != head_count:
        partials = lax.dot_general(
            (gated * inv_scale[:, None]).astype(jnp.bfloat16),
            lax.all_gather(out_weight, "seq", axis=0, tiled=True),
            contract,
            preferred_element_type=f32,
        )
        summed = lax.psum_scatter(partials, "head", scatter_dimension=1, tiled=True)
        return summed.astype(jnp.bfloat16)

    gated = gated.astype(jnp.bfloat16)
    swap = [
        (s * head_count + h, h * head_count + s)
        for s in range(seq_count)
        for h in range(head_count)
    ]
    rows = tok_rows // CHUNKS
    pieces = []
    for c in range(CHUNKS):
        everyone = lax.all_gather(gated[c * rows : (c + 1) * rows], "seq", axis=0, tiled=True)
        partials = lax.dot_general(everyone, out_weight, contract, preferred_element_type=f32)
        summed = lax.psum_scatter(
            partials.astype(jnp.bfloat16), "head", scatter_dimension=0, tiled=True
        )
        pieces.append(lax.ppermute(summed, ("seq", "head"), swap))
    out = jnp.concatenate(pieces, axis=0).astype(f32) * inv_scale[:, None]
    return out.astype(jnp.bfloat16)


def solution(mesh):
    split = P(("groups", "seq"), "head")
    in_specs = (split, split, split, split, P("head"), P("head"), P("groups"), P("seq", "head"))
    return jax.shard_map(shards, mesh=mesh, in_specs=in_specs, out_specs=split, check_vma=False)
```

```python
import jax
import jax.numpy as jnp
from jax import lax
from jax.sharding import PartitionSpec as P

HEAD_DIM = 128
CHUNKS = 2


def doc_positions(doc_lengths, position):
    order = jnp.arange(doc_lengths.shape[0], dtype=jnp.int32)
    starts = jnp.sum(jnp.where(order[None, :] < order[:, None], doc_lengths[None, :], 0), axis=1)
    doc_begin = jnp.max(jnp.where(starts[None, :] <= position[:, None], starts[None, :], 0), axis=1)
    return position - doc_begin


def shards(
    layer_queries,
    layer_keys,
    layer_values,
    gate_logits,
    norm_gain,
    decay_exponents,
    doc_lengths,
    out_weight,
):
    f32 = jnp.float32
    tok_rows = layer_queries.shape[0]
    heads_here = decay_exponents.shape[0]
    seq_count, head_count = lax.axis_size("seq"), lax.axis_size("head")
    mine = lax.axis_index("seq")
    token_span = tok_rows * seq_count
    decay_rate = jnp.minimum(jnp.exp2(decay_exponents.astype(f32)) / token_span, 1.0 / 32.0)
    local_pos = jnp.arange(tok_rows, dtype=jnp.int32)
    within = doc_positions(doc_lengths, mine * tok_rows + local_pos)
    last_within = within[tok_rows - 1]
    query_heads = layer_queries.reshape(tok_rows, heads_here, HEAD_DIM)
    key_heads = layer_keys.reshape(tok_rows, heads_here, HEAD_DIM)
    value_heads = layer_values.reshape(tok_rows, heads_here, HEAD_DIM)

    key_weight = jnp.where(
        (local_pos >= tok_rows - 1 - last_within)[:, None],
        jnp.exp(-decay_rate[None, :] * (tok_rows - local_pos)[:, None].astype(f32)),
        0.0,
    )
    scaled = (key_heads.astype(f32) * key_weight[:, :, None]).astype(jnp.bfloat16)
    block_state = jnp.einsum("thd,the->hde", scaled, value_heads, preferred_element_type=f32)
    direct = seq_count == head_count and head_count & (head_count - 1) == 0 and head_count > 1
    sent_state = block_state.astype(jnp.bfloat16)
    if direct:
        states = [
            lax.ppermute(sent_state, "seq", [(s, s + k) for s in range(seq_count - k)])
            for k in range(1, seq_count)
        ]
    else:
        states = lax.all_gather(sent_state, "seq")

    blocks = jnp.arange(seq_count, dtype=jnp.int32)
    ends = doc_positions(doc_lengths, blocks * tok_rows + tok_rows - 1)
    carry = jnp.where(
        (ends >= tok_rows)[:, None], jnp.exp(-decay_rate * tok_rows)[None, :], 0.0
    )
    between = (blocks[None, :] > blocks[:, None]) & (blocks[None, :] < mine)
    reach = jnp.prod(jnp.where(between[:, :, None], carry[None], 1.0), axis=1)
    reach = jnp.where((blocks < mine)[:, None], reach, 0.0)

    lag_grid = local_pos[:, None] - local_pos[None, :]
    valid_mask = (lag_grid >= 0) & (lag_grid <= within[:, None])
    decay_grid = jnp.where(
        valid_mask[None], jnp.exp(-decay_rate[:, None, None] * lag_grid[None].astype(f32)), 0.0
    )
    scores = jnp.einsum("thd,shd->hts", query_heads, key_heads, preferred_element_type=f32)
    weights = (scores * decay_grid).astype(jnp.bfloat16)
    intra_attn = jnp.einsum("hts,shd->thd", weights, value_heads, preferred_element_type=f32)
    if direct:
        incoming = jnp.zeros_like(block_state)
        for k in range(1, seq_count):
            far = jnp.where(mine >= k, reach[jnp.maximum(mine - k, 0)], 0.0)
            incoming += far[:, None, None] * states[k - 1].astype(f32)
    else:
        incoming = jnp.sum(reach[:, :, None, None] * states.astype(f32), axis=0)
    query_weight = jnp.where(
        (within >= local_pos + 1)[:, None],
        jnp.exp(-decay_rate[None, :] * local_pos[:, None].astype(f32)),
        0.0,
    )
    cross_attn = (
        jnp.einsum(
            "thd,hde->the",
            query_heads,
            incoming.astype(jnp.bfloat16),
            preferred_element_type=f32,
        )
        * query_weight[:, :, None]
    )
    attention = (intra_attn + cross_attn).reshape(tok_rows, heads_here * HEAD_DIM)
    squares = jnp.sum(attention * attention, axis=1)
    if direct:
        step = 1
        while step < head_count:
            squares += lax.ppermute(squares, "head", [(h, h ^ step) for h in range(head_count)])
            step *= 2
    else:
        squares = lax.psum(squares, "head")
    inv_scale = lax.rsqrt(squares / (heads_here * HEAD_DIM * head_count) + 1e-06)
    gated = attention * norm_gain.astype(f32) * jax.nn.sigmoid(gate_logits.astype(f32))
    contract = (((1,), (1,)), ((), ()))

    if not direct:
        partials = lax.dot_general(
            (gated * inv_scale[:, None]).astype(jnp.bfloat16),
            lax.all_gather(out_weight, "seq", axis=0, tiled=True),
            contract,
            preferred_element_type=f32,
        )
        summed = lax.psum_scatter(partials, "head", scatter_dimension=1, tiled=True)
        return summed.astype(jnp.bfloat16)

    gated = gated.astype(jnp.bfloat16)
    head = lax.axis_index("head")
    same = (mine % 2) == (head % 2)
    pairs = seq_count // 2
    rows = tok_rows // CHUNKS
    pieces = []
    for c in range(CHUNKS):
        part = gated[c * rows : (c + 1) * rows]
        given = [part] + [
            lax.ppermute(part, "seq", [(s, s ^ k) for s in range(seq_count)])
            for k in range(1, seq_count)
        ]
        reduced = []
        for p in range(pairs):
            here, there = given[2 * p], given[2 * p + 1]
            other = lax.dot_general(
                jnp.where(same, there, here), out_weight, contract, preferred_element_type=f32
            ).astype(jnp.bfloat16)
            came = lax.ppermute(other, "head", [(h, h ^ 1) for h in range(head_count)])
            kept = lax.dot_general(
                jnp.where(same, here, there), out_weight, contract, preferred_element_type=f32
            )
            reduced.append((kept + came.astype(f32)).astype(jnp.bfloat16))
        total = jnp.zeros(reduced[0].shape, f32)
        for j in range(pairs):
            pick = jnp.bitwise_xor(jnp.bitwise_xor(mine // 2, head // 2), j)
            chosen = reduced[0]
            for p in range(1, pairs):
                chosen = jnp.where(pick == p, reduced[p], chosen)
            route = [
                (s * head_count + h, (h ^ (2 * j)) * head_count + s)
                for s in range(seq_count)
                for h in range(head_count)
            ]
            total += lax.ppermute(chosen, ("seq", "head"), route).astype(f32)
        pieces.append(total)
    out = jnp.concatenate(pieces, axis=0) * inv_scale[:, None]
    return out.astype(jnp.bfloat16)


def solution(mesh):
    split = P(("groups", "seq"), "head")
    in_specs = (split, split, split, split, P("head"), P("head"), P("groups"), P("seq", "head"))
    return jax.shard_map(shards, mesh=mesh, in_specs=in_specs, out_specs=split, check_vma=False)
```

```python
import functools

import jax
import jax.numpy as jnp
from jax import lax
from jax.experimental import pallas as pl
from jax.experimental.pallas import tpu as pltpu
from jax.sharding import PartitionSpec as P

HEAD_DIM = 128
CHUNKS = 4

MESH = pl.DeviceIdType.MESH


def project_kernel(
    count, g_ref, w_ref, out_ref, given, send0, recv0, send1, recv1, hold, send2,
    hop_send, hop_recv, pair_send, pair_recv, swap_send, swap_recv,
):
    me, head = lax.axis_index("seq"), lax.axis_index("head")
    core, across = head % 2, head // 2
    mate = head + 1 - 2 * core
    far = (1 - across) * 2 + core
    rows = g_ref.shape[0] // CHUNKS
    width = w_ref.shape[0]
    tile = width // 3 if width % 384 == 0 else width

    barrier = pltpu.get_barrier_semaphore()

    def greet(**where):
        pl.semaphore_signal(barrier, inc=1, device_id=where, device_id_type=MESH)

    greet(head=mate)
    greet(head=far)
    pl.when(me > 0)(lambda: greet(seq=me - 1))
    pl.when(me < count - 1)(lambda: greet(seq=me + 1))
    pl.when(me != head)(lambda: greet(seq=head, head=me))
    apart, square = (me - head) * (me - head), count * count
    before, after = (me + count - 1) // count, (2 * count - 2 - me) // count
    pl.semaphore_wait(barrier, 2 + before + after + (apart + square - 1) // square)

    def hop(way, k, c):
        block = me - (k - 1) if way == 0 else me + (k - 1)
        part = pl.ds(c * rows, rows)
        src = g_ref.at[part] if k == 1 else given.at[block, part]
        return pltpu.make_async_remote_copy(
            src_ref=src,
            dst_ref=given.at[block, part],
            send_sem=hop_send.at[way, k - 1, c],
            recv_sem=hop_recv.at[way, k - 1, c],
            device_id={"seq": me + 1 if way == 0 else me - 1},
            device_id_type=MESH,
        )

    def arrival(way, k, c):
        block = me - k if way == 0 else me + k
        part = pl.ds(c * rows, rows)
        return pltpu.make_async_remote_copy(
            src_ref=given.at[block, part],
            dst_ref=given.at[block, part],
            send_sem=hop_send.at[way, k - 1, c],
            recv_sem=hop_recv.at[way, k - 1, c],
            device_id={"seq": me + 1 if way == 0 else me - 1},
            device_id_type=MESH,
        )

    def sends(way, k):
        if way == 0:
            return (me >= k - 1) & (me < count - 1)
        return (me <= count - k) & (me > 0)

    def comes(way, k):
        return me >= k if way == 0 else me < count - k

    def start_hop(k, c):
        for way in (0, 1):
            pl.when(sends(way, k))(lambda way=way: hop(way, k, c).start())

    def pair_copy(stage, slot, c):
        src, dst, to = (send1, recv1, far) if stage else (send0, recv0, mate)
        src, dst = (src.at[c], dst.at[c]) if stage else (src.at[c, slot], dst.at[c, slot])
        lane = 2 if stage else slot
        return pltpu.make_async_remote_copy(
            src_ref=src, dst_ref=dst,
            send_sem=pair_send.at[lane, c], recv_sem=pair_recv.at[lane, c],
            device_id={"head": to}, device_id_type=MESH,
        )

    def swap_copy(c):
        return pltpu.make_async_remote_copy(
            src_ref=send2.at[c], dst_ref=out_ref.at[pl.ds(c * rows, rows)],
            send_sem=swap_send.at[c], recv_sem=swap_recv.at[c],
            device_id={"seq": head, "head": me}, device_id_type=MESH,
        )

    def product(block, c, put):
        @pl.loop(0, width // tile)
        def _(i):
            span = pl.ds(pl.multiple_of(i * tile, 128), tile)
            put(span, lax.dot_general(
                given[block, pl.ds(c * rows, rows), :], w_ref[span, :],
                (((1,), (1,)), ((), ())), preferred_element_type=jnp.float32,
            ))

    def finish(c):
        pair_copy(1, 0, c).wait_recv()
        send2[c] = (hold[c] + recv1[c].astype(jnp.float32)).astype(jnp.bfloat16)

        @pl.when(me != head)
        def _():
            swap_copy(c).start()

        @pl.when(me == head)
        def _():
            out_ref[pl.ds(c * rows, rows), :] = send2[c]

    start_hop(1, 0)
    start_hop(1, 1)
    given[me] = g_ref[...]
    for c in range(CHUNKS):
        for k in range(1, count):
            for way in (0, 1):
                pl.when(comes(way, k))(lambda way=way: arrival(way, k, c).wait_recv())
            if k < count - 1:
                start_hop(k + 1, c)
        if c + 2 < CHUNKS:
            start_hop(1, c + 2)

        for slot in range(2):
            def put_other(span, value):
                send0[c, slot, :, span] = value.astype(jnp.bfloat16)

            side = 1 - across if slot == 0 else across
            product(2 * side + 1 - core, c, put_other)
            pair_copy(0, slot, c).start()

        pair_copy(0, 0, c).wait_recv()

        def put_far(span, value):
            total = value + recv0[c, 0, :, span].astype(jnp.float32)
            send1[c, :, span] = total.astype(jnp.bfloat16)

        product(far, c, put_far)
        pair_copy(1, 0, c).start()
        pair_copy(0, 1, c).wait_recv()

        def put_mine(span, value):
            hold[c, :, span] = value + recv0[c, 1, :, span].astype(jnp.float32)

        product(head, c, put_mine)
        if c > 0:
            finish(c - 1)
    finish(CHUNKS - 1)
    for c in range(CHUNKS):
        for k in range(1, count):
            for way in (0, 1):
                pl.when(sends(way, k))(lambda way=way: hop(way, k, c).wait_send())
        for slot in range(2):
            pair_copy(0, slot, c).wait_send()
        pair_copy(1, 0, c).wait_send()

        @pl.when(me != head)
        def _():
            swap_copy(c).wait()


def project(gated, out_weight, count):
    tok_rows, depth = gated.shape
    width = out_weight.shape[0]
    rows = tok_rows // CHUNKS
    half = functools.partial(pltpu.VMEM, dtype=jnp.bfloat16)
    return pl.pallas_call(
        functools.partial(project_kernel, count),
        out_shape=jax.ShapeDtypeStruct((tok_rows, width), jnp.bfloat16),
        in_specs=[pl.BlockSpec(memory_space=pltpu.VMEM)] * 2,
        out_specs=pl.BlockSpec(memory_space=pltpu.VMEM),
        scratch_shapes=[
            half((count, tok_rows, depth)),
            half((CHUNKS, 2, rows, width)),
            half((CHUNKS, 2, rows, width)),
            half((CHUNKS, rows, width)),
            half((CHUNKS, rows, width)),
            pltpu.VMEM((CHUNKS, rows, width), jnp.float32),
            half((CHUNKS, rows, width)),
            pltpu.SemaphoreType.DMA((2, count - 1, CHUNKS)),
            pltpu.SemaphoreType.DMA((2, count - 1, CHUNKS)),
            pltpu.SemaphoreType.DMA((3, CHUNKS)),
            pltpu.SemaphoreType.DMA((3, CHUNKS)),
            pltpu.SemaphoreType.DMA((CHUNKS,)),
            pltpu.SemaphoreType.DMA((CHUNKS,)),
        ],
        compiler_params=pltpu.CompilerParams(
            collective_id=0, has_side_effects=True, vmem_limit_bytes=48 * 1024 * 1024
        ),
        cost_estimate=pl.CostEstimate(
            flops=2 * count * tok_rows * depth * width,
            bytes_accessed=2 * (tok_rows * depth + width * depth + tok_rows * width),
            transcendentals=0,
        ),
    )(gated, out_weight)


def doc_positions(doc_lengths, position):
    order = jnp.arange(doc_lengths.shape[0], dtype=jnp.int32)
    starts = jnp.sum(jnp.where(order[None, :] < order[:, None], doc_lengths[None, :], 0), axis=1)
    doc_begin = jnp.max(jnp.where(starts[None, :] <= position[:, None], starts[None, :], 0), axis=1)
    return position - doc_begin


def shards(
    layer_queries,
    layer_keys,
    layer_values,
    gate_logits,
    norm_gain,
    decay_exponents,
    doc_lengths,
    out_weight,
):
    f32 = jnp.float32
    tok_rows = layer_queries.shape[0]
    heads_here = decay_exponents.shape[0]
    seq_count, head_count = lax.axis_size("seq"), lax.axis_size("head")
    mine = lax.axis_index("seq")
    token_span = tok_rows * seq_count
    decay_rate = jnp.minimum(jnp.exp2(decay_exponents.astype(f32)) / token_span, 1.0 / 32.0)
    local_pos = jnp.arange(tok_rows, dtype=jnp.int32)
    within = doc_positions(doc_lengths, mine * tok_rows + local_pos)
    last_within = within[tok_rows - 1]
    query_heads = layer_queries.reshape(tok_rows, heads_here, HEAD_DIM)
    key_heads = layer_keys.reshape(tok_rows, heads_here, HEAD_DIM)
    value_heads = layer_values.reshape(tok_rows, heads_here, HEAD_DIM)

    key_weight = jnp.where(
        (local_pos >= tok_rows - 1 - last_within)[:, None],
        jnp.exp(-decay_rate[None, :] * (tok_rows - local_pos)[:, None].astype(f32)),
        0.0,
    )
    scaled = (key_heads.astype(f32) * key_weight[:, :, None]).astype(jnp.bfloat16)
    block_state = jnp.einsum("thd,the->hde", scaled, value_heads, preferred_element_type=f32)
    direct = seq_count == head_count and head_count // 2 == 2 and head_count % 2 == 0
    sent_state = block_state.astype(jnp.bfloat16)
    if direct:
        states = [
            lax.ppermute(sent_state, "seq", [(s, s + k) for s in range(seq_count - k)])
            for k in range(1, seq_count)
        ]
    else:
        states = lax.all_gather(sent_state, "seq")

    blocks = jnp.arange(seq_count, dtype=jnp.int32)
    ends = doc_positions(doc_lengths, blocks * tok_rows + tok_rows - 1)
    carry = jnp.where(
        (ends >= tok_rows)[:, None], jnp.exp(-decay_rate * tok_rows)[None, :], 0.0
    )
    between = (blocks[None, :] > blocks[:, None]) & (blocks[None, :] < mine)
    reach = jnp.prod(jnp.where(between[:, :, None], carry[None], 1.0), axis=1)
    reach = jnp.where((blocks < mine)[:, None], reach, 0.0)

    lag_grid = local_pos[:, None] - local_pos[None, :]
    valid_mask = (lag_grid >= 0) & (lag_grid <= within[:, None])
    decay_grid = jnp.where(
        valid_mask[None], jnp.exp(-decay_rate[:, None, None] * lag_grid[None].astype(f32)), 0.0
    )
    scores = jnp.einsum("thd,shd->hts", query_heads, key_heads, preferred_element_type=f32)
    weights = (scores * decay_grid).astype(jnp.bfloat16)
    intra_attn = jnp.einsum("hts,shd->thd", weights, value_heads, preferred_element_type=f32)
    if direct:
        incoming = jnp.zeros_like(block_state)
        for k in range(1, seq_count):
            far = jnp.where(mine >= k, reach[jnp.maximum(mine - k, 0)], 0.0)
            incoming += far[:, None, None] * states[k - 1].astype(f32)
    else:
        incoming = jnp.sum(reach[:, :, None, None] * states.astype(f32), axis=0)
    query_weight = jnp.where(
        (within >= local_pos + 1)[:, None],
        jnp.exp(-decay_rate[None, :] * local_pos[:, None].astype(f32)),
        0.0,
    )
    cross_attn = (
        jnp.einsum(
            "thd,hde->the",
            query_heads,
            incoming.astype(jnp.bfloat16),
            preferred_element_type=f32,
        )
        * query_weight[:, :, None]
    )
    attention = (intra_attn + cross_attn).reshape(tok_rows, heads_here * HEAD_DIM)
    squares = jnp.sum(attention * attention, axis=1)
    if direct:
        step = 1
        while step < head_count:
            squares += lax.ppermute(squares, "head", [(h, h ^ step) for h in range(head_count)])
            step *= 2
    else:
        squares = lax.psum(squares, "head")
    inv_scale = lax.rsqrt(squares / (heads_here * HEAD_DIM * head_count) + 1e-06)
    gated = attention * norm_gain.astype(f32) * jax.nn.sigmoid(gate_logits.astype(f32))
    contract = (((1,), (1,)), ((), ()))

    if not direct:
        partials = lax.dot_general(
            (gated * inv_scale[:, None]).astype(jnp.bfloat16),
            lax.all_gather(out_weight, "seq", axis=0, tiled=True),
            contract,
            preferred_element_type=f32,
        )
        summed = lax.psum_scatter(partials, "head", scatter_dimension=1, tiled=True)
        return summed.astype(jnp.bfloat16)

    gated = gated.astype(jnp.bfloat16)
    out = project(gated, out_weight, seq_count).astype(f32) * inv_scale[:, None]
    return out.astype(jnp.bfloat16)


def solution(mesh):
    split = P(("groups", "seq"), "head")
    in_specs = (split, split, split, split, P("head"), P("head"), P("groups"), P("seq", "head"))
    return jax.shard_map(shards, mesh=mesh, in_specs=in_specs, out_specs=split, check_vma=False)
```

```python
import functools

import jax
import jax.numpy as jnp
from jax import lax
from jax.experimental import pallas as pl
from jax.experimental.pallas import tpu as pltpu
from jax.sharding import PartitionSpec as P

HEAD_DIM = 128
CHUNKS = 4

MESH = pl.DeviceIdType.MESH


def project_kernel(
    count, g_ref, w_ref, out_ref, given, send0, recv0, send1, recv1, hold, send2,
    hop_send, hop_recv, pair_send, pair_recv, swap_send, swap_recv,
):
    me, head = lax.axis_index("seq"), lax.axis_index("head")
    core, across = head % 2, head // 2
    mate = head + 1 - 2 * core
    far = (1 - across) * 2 + core
    rows = g_ref.shape[0] // CHUNKS
    width = w_ref.shape[0]
    tile = width // 3 if width % 384 == 0 else width

    barrier = pltpu.get_barrier_semaphore()

    def greet(**where):
        pl.semaphore_signal(barrier, inc=1, device_id=where, device_id_type=MESH)

    greet(head=mate)
    greet(head=far)
    pl.when(me > 0)(lambda: greet(seq=me - 1))
    pl.when(me < count - 1)(lambda: greet(seq=me + 1))
    pl.when(me != head)(lambda: greet(seq=head, head=me))
    apart, square = (me - head) * (me - head), count * count
    before, after = (me + count - 1) // count, (2 * count - 2 - me) // count
    pl.semaphore_wait(barrier, 2 + before + after + (apart + square - 1) // square)

    def hop(way, k, c):
        block = me - (k - 1) if way == 0 else me + (k - 1)
        part = pl.ds(c * rows, rows)
        src = g_ref.at[part] if k == 1 else given.at[block, part]
        return pltpu.make_async_remote_copy(
            src_ref=src,
            dst_ref=given.at[block, part],
            send_sem=hop_send.at[way, k - 1, c],
            recv_sem=hop_recv.at[way, k - 1, c],
            device_id={"seq": me + 1 if way == 0 else me - 1},
            device_id_type=MESH,
        )

    def arrival(way, k, c):
        block = me - k if way == 0 else me + k
        part = pl.ds(c * rows, rows)
        return pltpu.make_async_remote_copy(
            src_ref=given.at[block, part],
            dst_ref=given.at[block, part],
            send_sem=hop_send.at[way, k - 1, c],
            recv_sem=hop_recv.at[way, k - 1, c],
            device_id={"seq": me + 1 if way == 0 else me - 1},
            device_id_type=MESH,
        )

    def sends(way, k):
        if way == 0:
            return (me >= k - 1) & (me < count - 1)
        return (me <= count - k) & (me > 0)

    def comes(way, k):
        return me >= k if way == 0 else me < count - k

    def start_hop(k, c):
        for way in (0, 1):
            pl.when(sends(way, k))(lambda way=way: hop(way, k, c).start())

    def pair_copy(stage, slot, c):
        src, dst, to = (send1, recv1, far) if stage else (send0, recv0, mate)
        src, dst = (src.at[c], dst.at[c]) if stage else (src.at[c, slot], dst.at[c, slot])
        lane = 2 if stage else slot
        return pltpu.make_async_remote_copy(
            src_ref=src, dst_ref=dst,
            send_sem=pair_send.at[lane, c], recv_sem=pair_recv.at[lane, c],
            device_id={"head": to}, device_id_type=MESH,
        )

    def swap_copy(c):
        return pltpu.make_async_remote_copy(
            src_ref=send2.at[c], dst_ref=out_ref.at[pl.ds(c * rows, rows)],
            send_sem=swap_send.at[c], recv_sem=swap_recv.at[c],
            device_id={"seq": head, "head": me}, device_id_type=MESH,
        )

    def product(block, c, put):
        @pl.loop(0, width // tile)
        def _(i):
            span = pl.ds(pl.multiple_of(i * tile, 128), tile)
            put(span, lax.dot_general(
                given[block, pl.ds(c * rows, rows), :], w_ref[span, :],
                (((1,), (1,)), ((), ())), preferred_element_type=jnp.float32,
            ))

    def finish(c):
        pair_copy(1, 0, c).wait_recv()
        send2[c] = (hold[c] + recv1[c].astype(jnp.float32)).astype(jnp.bfloat16)

        @pl.when(me != head)
        def _():
            swap_copy(c).start()

        @pl.when(me == head)
        def _():
            out_ref[pl.ds(c * rows, rows), :] = send2[c]

    def pump(k, c):
        for way in (0, 1):
            pl.when(comes(way, k))(lambda way=way: arrival(way, k, c).wait_recv())
        if k < count - 1:
            start_hop(k + 1, c)

    for c in range(CHUNKS):
        start_hop(1, c)
    given[me] = g_ref[...]
    for k in range(1, count - 1):
        pump(k, 0)
    for c in range(CHUNKS):
        pump(count - 1, c)
        if c + 1 < CHUNKS:
            pump(1, c + 1)

        for slot in range(2):
            def put_other(span, value):
                send0[c, slot, :, span] = value.astype(jnp.bfloat16)

            side = 1 - across if slot == 0 else across
            product(2 * side + 1 - core, c, put_other)
            pair_copy(0, slot, c).start()

        if c + 1 < CHUNKS:
            for k in range(2, count - 1):
                pump(k, c + 1)
        pair_copy(0, 0, c).wait_recv()

        def put_far(span, value):
            total = value + recv0[c, 0, :, span].astype(jnp.float32)
            send1[c, :, span] = total.astype(jnp.bfloat16)

        product(far, c, put_far)
        pair_copy(1, 0, c).start()
        pair_copy(0, 1, c).wait_recv()

        def put_mine(span, value):
            hold[c, :, span] = value + recv0[c, 1, :, span].astype(jnp.float32)

        product(head, c, put_mine)
        if c > 0:
            finish(c - 1)
    finish(CHUNKS - 1)
    for c in range(CHUNKS):
        for k in range(1, count):
            for way in (0, 1):
                pl.when(sends(way, k))(lambda way=way: hop(way, k, c).wait_send())
        for slot in range(2):
            pair_copy(0, slot, c).wait_send()
        pair_copy(1, 0, c).wait_send()

        @pl.when(me != head)
        def _():
            swap_copy(c).wait()


def project(gated, out_weight, count):
    tok_rows, depth = gated.shape
    width = out_weight.shape[0]
    rows = tok_rows // CHUNKS
    half = functools.partial(pltpu.VMEM, dtype=jnp.bfloat16)
    return pl.pallas_call(
        functools.partial(project_kernel, count),
        out_shape=jax.ShapeDtypeStruct((tok_rows, width), jnp.bfloat16),
        in_specs=[pl.BlockSpec(memory_space=pltpu.VMEM)] * 2,
        out_specs=pl.BlockSpec(memory_space=pltpu.VMEM),
        scratch_shapes=[
            half((count, tok_rows, depth)),
            half((CHUNKS, 2, rows, width)),
            half((CHUNKS, 2, rows, width)),
            half((CHUNKS, rows, width)),
            half((CHUNKS, rows, width)),
            pltpu.VMEM((CHUNKS, rows, width), jnp.float32),
            half((CHUNKS, rows, width)),
            pltpu.SemaphoreType.DMA((2, count - 1, CHUNKS)),
            pltpu.SemaphoreType.DMA((2, count - 1, CHUNKS)),
            pltpu.SemaphoreType.DMA((3, CHUNKS)),
            pltpu.SemaphoreType.DMA((3, CHUNKS)),
            pltpu.SemaphoreType.DMA((CHUNKS,)),
            pltpu.SemaphoreType.DMA((CHUNKS,)),
        ],
        compiler_params=pltpu.CompilerParams(
            collective_id=0, has_side_effects=True, vmem_limit_bytes=48 * 1024 * 1024
        ),
        cost_estimate=pl.CostEstimate(
            flops=2 * count * tok_rows * depth * width,
            bytes_accessed=2 * (tok_rows * depth + width * depth + tok_rows * width),
            transcendentals=0,
        ),
    )(gated, out_weight)


def doc_positions(doc_lengths, position):
    order = jnp.arange(doc_lengths.shape[0], dtype=jnp.int32)
    starts = jnp.sum(jnp.where(order[None, :] < order[:, None], doc_lengths[None, :], 0), axis=1)
    doc_begin = jnp.max(jnp.where(starts[None, :] <= position[:, None], starts[None, :], 0), axis=1)
    return position - doc_begin


def shards(
    layer_queries,
    layer_keys,
    layer_values,
    gate_logits,
    norm_gain,
    decay_exponents,
    doc_lengths,
    out_weight,
):
    f32 = jnp.float32
    tok_rows = layer_queries.shape[0]
    heads_here = decay_exponents.shape[0]
    seq_count, head_count = lax.axis_size("seq"), lax.axis_size("head")
    mine = lax.axis_index("seq")
    token_span = tok_rows * seq_count
    decay_rate = jnp.minimum(jnp.exp2(decay_exponents.astype(f32)) / token_span, 1.0 / 32.0)
    local_pos = jnp.arange(tok_rows, dtype=jnp.int32)
    within = doc_positions(doc_lengths, mine * tok_rows + local_pos)
    last_within = within[tok_rows - 1]
    query_heads = layer_queries.reshape(tok_rows, heads_here, HEAD_DIM)
    key_heads = layer_keys.reshape(tok_rows, heads_here, HEAD_DIM)
    value_heads = layer_values.reshape(tok_rows, heads_here, HEAD_DIM)

    key_weight = jnp.where(
        (local_pos >= tok_rows - 1 - last_within)[:, None],
        jnp.exp(-decay_rate[None, :] * (tok_rows - local_pos)[:, None].astype(f32)),
        0.0,
    )
    scaled = (key_heads.astype(f32) * key_weight[:, :, None]).astype(jnp.bfloat16)
    block_state = jnp.einsum("thd,the->hde", scaled, value_heads, preferred_element_type=f32)
    direct = seq_count == head_count and head_count // 2 == 2 and head_count % 2 == 0
    sent_state = block_state.astype(jnp.bfloat16)
    if direct:
        states = [
            lax.ppermute(sent_state, "seq", [(s, s + k) for s in range(seq_count - k)])
            for k in range(1, seq_count)
        ]
    else:
        states = lax.all_gather(sent_state, "seq")

    blocks = jnp.arange(seq_count, dtype=jnp.int32)
    ends = doc_positions(doc_lengths, blocks * tok_rows + tok_rows - 1)
    carry = jnp.where(
        (ends >= tok_rows)[:, None], jnp.exp(-decay_rate * tok_rows)[None, :], 0.0
    )
    between = (blocks[None, :] > blocks[:, None]) & (blocks[None, :] < mine)
    reach = jnp.prod(jnp.where(between[:, :, None], carry[None], 1.0), axis=1)
    reach = jnp.where((blocks < mine)[:, None], reach, 0.0)

    lag_grid = local_pos[:, None] - local_pos[None, :]
    valid_mask = (lag_grid >= 0) & (lag_grid <= within[:, None])
    decay_grid = jnp.where(
        valid_mask[None], jnp.exp(-decay_rate[:, None, None] * lag_grid[None].astype(f32)), 0.0
    )
    scores = jnp.einsum("thd,shd->hts", query_heads, key_heads, preferred_element_type=f32)
    weights = (scores * decay_grid).astype(jnp.bfloat16)
    intra_attn = jnp.einsum("hts,shd->thd", weights, value_heads, preferred_element_type=f32)
    if direct:
        incoming = jnp.zeros_like(block_state)
        for k in range(1, seq_count):
            far = jnp.where(mine >= k, reach[jnp.maximum(mine - k, 0)], 0.0)
            incoming += far[:, None, None] * states[k - 1].astype(f32)
    else:
        incoming = jnp.sum(reach[:, :, None, None] * states.astype(f32), axis=0)
    query_weight = jnp.where(
        (within >= local_pos + 1)[:, None],
        jnp.exp(-decay_rate[None, :] * local_pos[:, None].astype(f32)),
        0.0,
    )
    cross_attn = (
        jnp.einsum(
            "thd,hde->the",
            query_heads,
            incoming.astype(jnp.bfloat16),
            preferred_element_type=f32,
        )
        * query_weight[:, :, None]
    )
    attention = (intra_attn + cross_attn).reshape(tok_rows, heads_here * HEAD_DIM)
    squares = jnp.sum(attention * attention, axis=1)
    if direct:
        step = 1
        while step < head_count:
            squares += lax.ppermute(squares, "head", [(h, h ^ step) for h in range(head_count)])
            step *= 2
    else:
        squares = lax.psum(squares, "head")
    inv_scale = lax.rsqrt(squares / (heads_here * HEAD_DIM * head_count) + 1e-06)
    gated = attention * norm_gain.astype(f32) * jax.nn.sigmoid(gate_logits.astype(f32))
    contract = (((1,), (1,)), ((), ()))

    if not direct:
        partials = lax.dot_general(
            (gated * inv_scale[:, None]).astype(jnp.bfloat16),
            lax.all_gather(out_weight, "seq", axis=0, tiled=True),
            contract,
            preferred_element_type=f32,
        )
        summed = lax.psum_scatter(partials, "head", scatter_dimension=1, tiled=True)
        return summed.astype(jnp.bfloat16)

    gated = gated.astype(jnp.bfloat16)
    out = project(gated, out_weight, seq_count).astype(f32) * inv_scale[:, None]
    return out.astype(jnp.bfloat16)


def solution(mesh):
    split = P(("groups", "seq"), "head")
    in_specs = (split, split, split, split, P("head"), P("head"), P("groups"), P("seq", "head"))
    return jax.shard_map(shards, mesh=mesh, in_specs=in_specs, out_specs=split, check_vma=False)
```

```python
import functools

import jax
import jax.numpy as jnp
from jax import lax
from jax.experimental import pallas as pl
from jax.experimental.pallas import tpu as pltpu
from jax.sharding import PartitionSpec as P

HEAD_DIM = 128
CHUNKS = 8

MESH = pl.DeviceIdType.MESH


def project_kernel(
    count, g_ref, w_ref, out_ref, given, send0, recv0, send1, recv1, hold, send2,
    hop_send, hop_recv, pair_send, pair_recv, swap_send, swap_recv,
):
    me, head = lax.axis_index("seq"), lax.axis_index("head")
    core, across = head % 2, head // 2
    mate = head + 1 - 2 * core
    far = (1 - across) * 2 + core
    rows = g_ref.shape[0] // CHUNKS
    width = w_ref.shape[0]
    tile = width // 3 if width % 384 == 0 else width

    barrier = pltpu.get_barrier_semaphore()

    def greet(**where):
        pl.semaphore_signal(barrier, inc=1, device_id=where, device_id_type=MESH)

    greet(head=mate)
    greet(head=far)
    pl.when(me > 0)(lambda: greet(seq=me - 1))
    pl.when(me < count - 1)(lambda: greet(seq=me + 1))
    pl.when(me != head)(lambda: greet(seq=head, head=me))
    apart, square = (me - head) * (me - head), count * count
    before, after = (me + count - 1) // count, (2 * count - 2 - me) // count
    pl.semaphore_wait(barrier, 2 + before + after + (apart + square - 1) // square)

    def hop(way, k, c):
        block = me - (k - 1) if way == 0 else me + (k - 1)
        part = pl.ds(c * rows, rows)
        src = g_ref.at[part] if k == 1 else given.at[block, part]
        return pltpu.make_async_remote_copy(
            src_ref=src,
            dst_ref=given.at[block, part],
            send_sem=hop_send.at[way, k - 1, c],
            recv_sem=hop_recv.at[way, k - 1, c],
            device_id={"seq": me + 1 if way == 0 else me - 1},
            device_id_type=MESH,
        )

    def arrival(way, k, c):
        block = me - k if way == 0 else me + k
        part = pl.ds(c * rows, rows)
        return pltpu.make_async_remote_copy(
            src_ref=given.at[block, part],
            dst_ref=given.at[block, part],
            send_sem=hop_send.at[way, k - 1, c],
            recv_sem=hop_recv.at[way, k - 1, c],
            device_id={"seq": me + 1 if way == 0 else me - 1},
            device_id_type=MESH,
        )

    def sends(way, k):
        if way == 0:
            return (me >= k - 1) & (me < count - 1)
        return (me <= count - k) & (me > 0)

    def comes(way, k):
        return me >= k if way == 0 else me < count - k

    def start_hop(k, c):
        for way in (0, 1):
            pl.when(sends(way, k))(lambda way=way: hop(way, k, c).start())

    def pair_copy(stage, slot, c):
        src, dst, to = (send1, recv1, far) if stage else (send0, recv0, mate)
        src, dst = (src.at[c], dst.at[c]) if stage else (src.at[c, slot], dst.at[c, slot])
        lane = 2 if stage else slot
        return pltpu.make_async_remote_copy(
            src_ref=src, dst_ref=dst,
            send_sem=pair_send.at[lane, c], recv_sem=pair_recv.at[lane, c],
            device_id={"head": to}, device_id_type=MESH,
        )

    def swap_copy(c):
        return pltpu.make_async_remote_copy(
            src_ref=send2.at[c], dst_ref=out_ref.at[pl.ds(c * rows, rows)],
            send_sem=swap_send.at[c], recv_sem=swap_recv.at[c],
            device_id={"seq": head, "head": me}, device_id_type=MESH,
        )

    def product(block, c, put):
        @pl.loop(0, width // tile)
        def _(i):
            span = pl.ds(pl.multiple_of(i * tile, 128), tile)
            put(span, lax.dot_general(
                given[block, pl.ds(c * rows, rows), :], w_ref[span, :],
                (((1,), (1,)), ((), ())), preferred_element_type=jnp.float32,
            ))

    def finish(c):
        pair_copy(1, 0, c).wait_recv()
        send2[c] = (hold[c] + recv1[c].astype(jnp.float32)).astype(jnp.bfloat16)

        @pl.when(me != head)
        def _():
            swap_copy(c).start()

        @pl.when(me == head)
        def _():
            out_ref[pl.ds(c * rows, rows), :] = send2[c]

    def pump(k, c):
        for way in (0, 1):
            pl.when(comes(way, k))(lambda way=way: arrival(way, k, c).wait_recv())
        if k < count - 1:
            start_hop(k + 1, c)

    for c in range(CHUNKS):
        start_hop(1, c)
    given[me] = g_ref[...]
    for k in range(1, count - 1):
        pump(k, 0)
    for c in range(CHUNKS):
        pump(count - 1, c)
        if c + 1 < CHUNKS:
            pump(1, c + 1)

        for slot in range(2):
            def put_other(span, value):
                send0[c, slot, :, span] = value.astype(jnp.bfloat16)

            side = 1 - across if slot == 0 else across
            product(2 * side + 1 - core, c, put_other)
            pair_copy(0, slot, c).start()

        if c + 1 < CHUNKS:
            for k in range(2, count - 1):
                pump(k, c + 1)
        pair_copy(0, 0, c).wait_recv()

        def put_far(span, value):
            total = value + recv0[c, 0, :, span].astype(jnp.float32)
            send1[c, :, span] = total.astype(jnp.bfloat16)

        product(far, c, put_far)
        pair_copy(1, 0, c).start()
        pair_copy(0, 1, c).wait_recv()

        def put_mine(span, value):
            hold[c, :, span] = value + recv0[c, 1, :, span].astype(jnp.float32)

        product(head, c, put_mine)
        if c > 0:
            finish(c - 1)
    finish(CHUNKS - 1)
    for c in range(CHUNKS):
        for k in range(1, count):
            for way in (0, 1):
                pl.when(sends(way, k))(lambda way=way: hop(way, k, c).wait_send())
        for slot in range(2):
            pair_copy(0, slot, c).wait_send()
        pair_copy(1, 0, c).wait_send()

        @pl.when(me != head)
        def _():
            swap_copy(c).wait()


def project(gated, out_weight, count):
    tok_rows, depth = gated.shape
    width = out_weight.shape[0]
    rows = tok_rows // CHUNKS
    half = functools.partial(pltpu.VMEM, dtype=jnp.bfloat16)
    return pl.pallas_call(
        functools.partial(project_kernel, count),
        out_shape=jax.ShapeDtypeStruct((tok_rows, width), jnp.bfloat16),
        in_specs=[pl.BlockSpec(memory_space=pltpu.VMEM)] * 2,
        out_specs=pl.BlockSpec(memory_space=pltpu.VMEM),
        scratch_shapes=[
            half((count, tok_rows, depth)),
            half((CHUNKS, 2, rows, width)),
            half((CHUNKS, 2, rows, width)),
            half((CHUNKS, rows, width)),
            half((CHUNKS, rows, width)),
            pltpu.VMEM((CHUNKS, rows, width), jnp.float32),
            half((CHUNKS, rows, width)),
            pltpu.SemaphoreType.DMA((2, count - 1, CHUNKS)),
            pltpu.SemaphoreType.DMA((2, count - 1, CHUNKS)),
            pltpu.SemaphoreType.DMA((3, CHUNKS)),
            pltpu.SemaphoreType.DMA((3, CHUNKS)),
            pltpu.SemaphoreType.DMA((CHUNKS,)),
            pltpu.SemaphoreType.DMA((CHUNKS,)),
        ],
        compiler_params=pltpu.CompilerParams(
            collective_id=0, has_side_effects=True, vmem_limit_bytes=48 * 1024 * 1024
        ),
        cost_estimate=pl.CostEstimate(
            flops=2 * count * tok_rows * depth * width,
            bytes_accessed=2 * (tok_rows * depth + width * depth + tok_rows * width),
            transcendentals=0,
        ),
    )(gated, out_weight)


def doc_positions(doc_lengths, position):
    order = jnp.arange(doc_lengths.shape[0], dtype=jnp.int32)
    starts = jnp.sum(jnp.where(order[None, :] < order[:, None], doc_lengths[None, :], 0), axis=1)
    doc_begin = jnp.max(jnp.where(starts[None, :] <= position[:, None], starts[None, :], 0), axis=1)
    return position - doc_begin


def shards(
    layer_queries,
    layer_keys,
    layer_values,
    gate_logits,
    norm_gain,
    decay_exponents,
    doc_lengths,
    out_weight,
):
    f32 = jnp.float32
    tok_rows = layer_queries.shape[0]
    heads_here = decay_exponents.shape[0]
    seq_count, head_count = lax.axis_size("seq"), lax.axis_size("head")
    mine = lax.axis_index("seq")
    token_span = tok_rows * seq_count
    decay_rate = jnp.minimum(jnp.exp2(decay_exponents.astype(f32)) / token_span, 1.0 / 32.0)
    local_pos = jnp.arange(tok_rows, dtype=jnp.int32)
    within = doc_positions(doc_lengths, mine * tok_rows + local_pos)
    last_within = within[tok_rows - 1]
    query_heads = layer_queries.reshape(tok_rows, heads_here, HEAD_DIM)
    key_heads = layer_keys.reshape(tok_rows, heads_here, HEAD_DIM)
    value_heads = layer_values.reshape(tok_rows, heads_here, HEAD_DIM)

    key_weight = jnp.where(
        (local_pos >= tok_rows - 1 - last_within)[:, None],
        jnp.exp(-decay_rate[None, :] * (tok_rows - local_pos)[:, None].astype(f32)),
        0.0,
    )
    scaled = (key_heads.astype(f32) * key_weight[:, :, None]).astype(jnp.bfloat16)
    block_state = jnp.einsum("thd,the->hde", scaled, value_heads, preferred_element_type=f32)
    direct = seq_count == head_count and head_count // 2 == 2 and head_count % 2 == 0
    sent_state = block_state.astype(jnp.bfloat16)
    if direct:
        states = [
            lax.ppermute(sent_state, "seq", [(s, s + k) for s in range(seq_count - k)])
            for k in range(1, seq_count)
        ]
    else:
        states = lax.all_gather(sent_state, "seq")

    blocks = jnp.arange(seq_count, dtype=jnp.int32)
    ends = doc_positions(doc_lengths, blocks * tok_rows + tok_rows - 1)
    carry = jnp.where(
        (ends >= tok_rows)[:, None], jnp.exp(-decay_rate * tok_rows)[None, :], 0.0
    )
    between = (blocks[None, :] > blocks[:, None]) & (blocks[None, :] < mine)
    reach = jnp.prod(jnp.where(between[:, :, None], carry[None], 1.0), axis=1)
    reach = jnp.where((blocks < mine)[:, None], reach, 0.0)

    lag_grid = local_pos[:, None] - local_pos[None, :]
    valid_mask = (lag_grid >= 0) & (lag_grid <= within[:, None])
    decay_grid = jnp.where(
        valid_mask[None], jnp.exp(-decay_rate[:, None, None] * lag_grid[None].astype(f32)), 0.0
    )
    scores = jnp.einsum("thd,shd->hts", query_heads, key_heads, preferred_element_type=f32)
    weights = (scores * decay_grid).astype(jnp.bfloat16)
    intra_attn = jnp.einsum("hts,shd->thd", weights, value_heads, preferred_element_type=f32)
    if direct:
        incoming = jnp.zeros_like(block_state)
        for k in range(1, seq_count):
            far = jnp.where(mine >= k, reach[jnp.maximum(mine - k, 0)], 0.0)
            incoming += far[:, None, None] * states[k - 1].astype(f32)
    else:
        incoming = jnp.sum(reach[:, :, None, None] * states.astype(f32), axis=0)
    query_weight = jnp.where(
        (within >= local_pos + 1)[:, None],
        jnp.exp(-decay_rate[None, :] * local_pos[:, None].astype(f32)),
        0.0,
    )
    cross_attn = (
        jnp.einsum(
            "thd,hde->the",
            query_heads,
            incoming.astype(jnp.bfloat16),
            preferred_element_type=f32,
        )
        * query_weight[:, :, None]
    )
    attention = (intra_attn + cross_attn).reshape(tok_rows, heads_here * HEAD_DIM)
    squares = jnp.sum(attention * attention, axis=1)
    if direct:
        step = 1
        while step < head_count:
            squares += lax.ppermute(squares, "head", [(h, h ^ step) for h in range(head_count)])
            step *= 2
    else:
        squares = lax.psum(squares, "head")
    inv_scale = lax.rsqrt(squares / (heads_here * HEAD_DIM * head_count) + 1e-06)
    gated = attention * norm_gain.astype(f32) * jax.nn.sigmoid(gate_logits.astype(f32))
    contract = (((1,), (1,)), ((), ()))

    if not direct:
        partials = lax.dot_general(
            (gated * inv_scale[:, None]).astype(jnp.bfloat16),
            lax.all_gather(out_weight, "seq", axis=0, tiled=True),
            contract,
            preferred_element_type=f32,
        )
        summed = lax.psum_scatter(partials, "head", scatter_dimension=1, tiled=True)
        return summed.astype(jnp.bfloat16)

    gated = gated.astype(jnp.bfloat16)
    out = project(gated, out_weight, seq_count).astype(f32) * inv_scale[:, None]
    return out.astype(jnp.bfloat16)


def solution(mesh):
    split = P(("groups", "seq"), "head")
    in_specs = (split, split, split, split, P("head"), P("head"), P("groups"), P("seq", "head"))
    return jax.shard_map(shards, mesh=mesh, in_specs=in_specs, out_specs=split, check_vma=False)
```

```python
import functools

import jax
import jax.numpy as jnp
from jax import lax
from jax.experimental import pallas as pl
from jax.experimental.pallas import tpu as pltpu
from jax.sharding import PartitionSpec as P

HEAD_DIM = 128
CHUNKS = 2

MESH = pl.DeviceIdType.MESH


def project_kernel(
    count, g_ref, w_ref, out_ref, given, send0, recv0, send1, recv1, hold, send2,
    hop_send, hop_recv, pair_send, pair_recv, swap_send, swap_recv,
):
    me, head = lax.axis_index("seq"), lax.axis_index("head")
    core, across = head % 2, head // 2
    mate = head + 1 - 2 * core
    far = (1 - across) * 2 + core
    rows = g_ref.shape[0] // CHUNKS
    width = w_ref.shape[0]
    tile = width // 3 if width % 384 == 0 else width

    barrier = pltpu.get_barrier_semaphore()

    def greet(**where):
        pl.semaphore_signal(barrier, inc=1, device_id=where, device_id_type=MESH)

    greet(head=mate)
    greet(head=far)
    pl.when(me > 0)(lambda: greet(seq=me - 1))
    pl.when(me < count - 1)(lambda: greet(seq=me + 1))
    pl.when(me != head)(lambda: greet(seq=head, head=me))
    apart, square = (me - head) * (me - head), count * count
    before, after = (me + count - 1) // count, (2 * count - 2 - me) // count
    pl.semaphore_wait(barrier, 2 + before + after + (apart + square - 1) // square)

    def hop(way, k, c):
        block = me - (k - 1) if way == 0 else me + (k - 1)
        part = pl.ds(c * rows, rows)
        src = g_ref.at[part] if k == 1 else given.at[block, part]
        return pltpu.make_async_remote_copy(
            src_ref=src,
            dst_ref=given.at[block, part],
            send_sem=hop_send.at[way, k - 1, c],
            recv_sem=hop_recv.at[way, k - 1, c],
            device_id={"seq": me + 1 if way == 0 else me - 1},
            device_id_type=MESH,
        )

    def arrival(way, k, c):
        block = me - k if way == 0 else me + k
        part = pl.ds(c * rows, rows)
        return pltpu.make_async_remote_copy(
            src_ref=given.at[block, part],
            dst_ref=given.at[block, part],
            send_sem=hop_send.at[way, k - 1, c],
            recv_sem=hop_recv.at[way, k - 1, c],
            device_id={"seq": me + 1 if way == 0 else me - 1},
            device_id_type=MESH,
        )

    def sends(way, k):
        if way == 0:
            return (me >= k - 1) & (me < count - 1)
        return (me <= count - k) & (me > 0)

    def comes(way, k):
        return me >= k if way == 0 else me < count - k

    def start_hop(k, c):
        for way in (0, 1):
            pl.when(sends(way, k))(lambda way=way: hop(way, k, c).start())

    def pair_copy(stage, slot, c):
        src, dst, to = (send1, recv1, far) if stage else (send0, recv0, mate)
        src, dst = (src.at[c], dst.at[c]) if stage else (src.at[c, slot], dst.at[c, slot])
        lane = 2 if stage else slot
        return pltpu.make_async_remote_copy(
            src_ref=src, dst_ref=dst,
            send_sem=pair_send.at[lane, c], recv_sem=pair_recv.at[lane, c],
            device_id={"head": to}, device_id_type=MESH,
        )

    def swap_copy(c):
        return pltpu.make_async_remote_copy(
            src_ref=send2.at[c], dst_ref=out_ref.at[pl.ds(c * rows, rows)],
            send_sem=swap_send.at[c], recv_sem=swap_recv.at[c],
            device_id={"seq": head, "head": me}, device_id_type=MESH,
        )

    def product(block, c, put):
        @pl.loop(0, width // tile)
        def _(i):
            span = pl.ds(pl.multiple_of(i * tile, 128), tile)
            put(span, lax.dot_general(
                given[block, pl.ds(c * rows, rows), :], w_ref[span, :],
                (((1,), (1,)), ((), ())), preferred_element_type=jnp.float32,
            ))

    def finish(c):
        pair_copy(1, 0, c).wait_recv()
        send2[c] = (hold[c] + recv1[c].astype(jnp.float32)).astype(jnp.bfloat16)

        @pl.when(me != head)
        def _():
            swap_copy(c).start()

        @pl.when(me == head)
        def _():
            out_ref[pl.ds(c * rows, rows), :] = send2[c]

    def pump(k, c):
        for way in (0, 1):
            pl.when(comes(way, k))(lambda way=way: arrival(way, k, c).wait_recv())
        if k < count - 1:
            start_hop(k + 1, c)

    for c in range(CHUNKS):
        start_hop(1, c)
    given[me] = g_ref[...]
    for k in range(1, count - 1):
        pump(k, 0)
    for c in range(CHUNKS):
        pump(count - 1, c)
        if c + 1 < CHUNKS:
            pump(1, c + 1)

        for slot in range(2):
            def put_other(span, value):
                send0[c, slot, :, span] = value.astype(jnp.bfloat16)

            side = 1 - across if slot == 0 else across
            product(2 * side + 1 - core, c, put_other)
            pair_copy(0, slot, c).start()

        if c + 1 < CHUNKS:
            for k in range(2, count - 1):
                pump(k, c + 1)
        pair_copy(0, 0, c).wait_recv()

        def put_far(span, value):
            total = value + recv0[c, 0, :, span].astype(jnp.float32)
            send1[c, :, span] = total.astype(jnp.bfloat16)

        product(far, c, put_far)
        pair_copy(1, 0, c).start()
        pair_copy(0, 1, c).wait_recv()

        def put_mine(span, value):
            hold[c, :, span] = value + recv0[c, 1, :, span].astype(jnp.float32)

        product(head, c, put_mine)
        if c > 0:
            finish(c - 1)
    finish(CHUNKS - 1)
    for c in range(CHUNKS):
        for k in range(1, count):
            for way in (0, 1):
                pl.when(sends(way, k))(lambda way=way: hop(way, k, c).wait_send())
        for slot in range(2):
            pair_copy(0, slot, c).wait_send()
        pair_copy(1, 0, c).wait_send()

        @pl.when(me != head)
        def _():
            swap_copy(c).wait()


def project(gated, out_weight, count):
    tok_rows, depth = gated.shape
    width = out_weight.shape[0]
    rows = tok_rows // CHUNKS
    half = functools.partial(pltpu.VMEM, dtype=jnp.bfloat16)
    return pl.pallas_call(
        functools.partial(project_kernel, count),
        out_shape=jax.ShapeDtypeStruct((tok_rows, width), jnp.bfloat16),
        in_specs=[pl.BlockSpec(memory_space=pltpu.VMEM)] * 2,
        out_specs=pl.BlockSpec(memory_space=pltpu.VMEM),
        scratch_shapes=[
            half((count, tok_rows, depth)),
            half((CHUNKS, 2, rows, width)),
            half((CHUNKS, 2, rows, width)),
            half((CHUNKS, rows, width)),
            half((CHUNKS, rows, width)),
            pltpu.VMEM((CHUNKS, rows, width), jnp.float32),
            half((CHUNKS, rows, width)),
            pltpu.SemaphoreType.DMA((2, count - 1, CHUNKS)),
            pltpu.SemaphoreType.DMA((2, count - 1, CHUNKS)),
            pltpu.SemaphoreType.DMA((3, CHUNKS)),
            pltpu.SemaphoreType.DMA((3, CHUNKS)),
            pltpu.SemaphoreType.DMA((CHUNKS,)),
            pltpu.SemaphoreType.DMA((CHUNKS,)),
        ],
        compiler_params=pltpu.CompilerParams(
            collective_id=0, has_side_effects=True, vmem_limit_bytes=48 * 1024 * 1024
        ),
        cost_estimate=pl.CostEstimate(
            flops=2 * count * tok_rows * depth * width,
            bytes_accessed=2 * (tok_rows * depth + width * depth + tok_rows * width),
            transcendentals=0,
        ),
    )(gated, out_weight)


def doc_positions(doc_lengths, position):
    order = jnp.arange(doc_lengths.shape[0], dtype=jnp.int32)
    starts = jnp.sum(jnp.where(order[None, :] < order[:, None], doc_lengths[None, :], 0), axis=1)
    doc_begin = jnp.max(jnp.where(starts[None, :] <= position[:, None], starts[None, :], 0), axis=1)
    return position - doc_begin


def shards(
    layer_queries,
    layer_keys,
    layer_values,
    gate_logits,
    norm_gain,
    decay_exponents,
    doc_lengths,
    out_weight,
):
    f32 = jnp.float32
    tok_rows = layer_queries.shape[0]
    heads_here = decay_exponents.shape[0]
    seq_count, head_count = lax.axis_size("seq"), lax.axis_size("head")
    mine = lax.axis_index("seq")
    token_span = tok_rows * seq_count
    decay_rate = jnp.minimum(jnp.exp2(decay_exponents.astype(f32)) / token_span, 1.0 / 32.0)
    local_pos = jnp.arange(tok_rows, dtype=jnp.int32)
    within = doc_positions(doc_lengths, mine * tok_rows + local_pos)
    last_within = within[tok_rows - 1]
    query_heads = layer_queries.reshape(tok_rows, heads_here, HEAD_DIM)
    key_heads = layer_keys.reshape(tok_rows, heads_here, HEAD_DIM)
    value_heads = layer_values.reshape(tok_rows, heads_here, HEAD_DIM)

    key_weight = jnp.where(
        (local_pos >= tok_rows - 1 - last_within)[:, None],
        jnp.exp(-decay_rate[None, :] * (tok_rows - local_pos)[:, None].astype(f32)),
        0.0,
    )
    scaled = (key_heads.astype(f32) * key_weight[:, :, None]).astype(jnp.bfloat16)
    block_state = jnp.einsum("thd,the->hde", scaled, value_heads, preferred_element_type=f32)
    direct = seq_count == head_count and head_count // 2 == 2 and head_count % 2 == 0
    sent_state = block_state.astype(jnp.bfloat16)
    if direct:
        states = [
            lax.ppermute(sent_state, "seq", [(s, s + k) for s in range(seq_count - k)])
            for k in range(1, seq_count)
        ]
    else:
        states = lax.all_gather(sent_state, "seq")

    blocks = jnp.arange(seq_count, dtype=jnp.int32)
    ends = doc_positions(doc_lengths, blocks * tok_rows + tok_rows - 1)
    carry = jnp.where(
        (ends >= tok_rows)[:, None], jnp.exp(-decay_rate * tok_rows)[None, :], 0.0
    )
    between = (blocks[None, :] > blocks[:, None]) & (blocks[None, :] < mine)
    reach = jnp.prod(jnp.where(between[:, :, None], carry[None], 1.0), axis=1)
    reach = jnp.where((blocks < mine)[:, None], reach, 0.0)

    lag_grid = local_pos[:, None] - local_pos[None, :]
    valid_mask = (lag_grid >= 0) & (lag_grid <= within[:, None])
    decay_grid = jnp.where(
        valid_mask[None], jnp.exp(-decay_rate[:, None, None] * lag_grid[None].astype(f32)), 0.0
    )
    scores = jnp.einsum("thd,shd->hts", query_heads, key_heads, preferred_element_type=f32)
    weights = (scores * decay_grid).astype(jnp.bfloat16)
    intra_attn = jnp.einsum("hts,shd->thd", weights, value_heads, preferred_element_type=f32)
    if direct:
        incoming = jnp.zeros_like(block_state)
        for k in range(1, seq_count):
            far = jnp.where(mine >= k, reach[jnp.maximum(mine - k, 0)], 0.0)
            incoming += far[:, None, None] * states[k - 1].astype(f32)
    else:
        incoming = jnp.sum(reach[:, :, None, None] * states.astype(f32), axis=0)
    query_weight = jnp.where(
        (within >= local_pos + 1)[:, None],
        jnp.exp(-decay_rate[None, :] * local_pos[:, None].astype(f32)),
        0.0,
    )
    cross_attn = (
        jnp.einsum(
            "thd,hde->the",
            query_heads,
            incoming.astype(jnp.bfloat16),
            preferred_element_type=f32,
        )
        * query_weight[:, :, None]
    )
    attention = (intra_attn + cross_attn).reshape(tok_rows, heads_here * HEAD_DIM)
    squares = jnp.sum(attention * attention, axis=1)
    if direct:
        step = 1
        while step < head_count:
            squares += lax.ppermute(squares, "head", [(h, h ^ step) for h in range(head_count)])
            step *= 2
    else:
        squares = lax.psum(squares, "head")
    inv_scale = lax.rsqrt(squares / (heads_here * HEAD_DIM * head_count) + 1e-06)
    gated = attention * norm_gain.astype(f32) * jax.nn.sigmoid(gate_logits.astype(f32))
    contract = (((1,), (1,)), ((), ()))

    if not direct:
        partials = lax.dot_general(
            (gated * inv_scale[:, None]).astype(jnp.bfloat16),
            lax.all_gather(out_weight, "seq", axis=0, tiled=True),
            contract,
            preferred_element_type=f32,
        )
        summed = lax.psum_scatter(partials, "head", scatter_dimension=1, tiled=True)
        return summed.astype(jnp.bfloat16)

    gated = gated.astype(jnp.bfloat16)
    out = project(gated, out_weight, seq_count).astype(f32) * inv_scale[:, None]
    return out.astype(jnp.bfloat16)


def solution(mesh):
    split = P(("groups", "seq"), "head")
    in_specs = (split, split, split, split, P("head"), P("head"), P("groups"), P("seq", "head"))
    return jax.shard_map(shards, mesh=mesh, in_specs=in_specs, out_specs=split, check_vma=False)
```
